32 devices in a mesh: wide: 8 (over z, core), narrow: 4 (over y, x).
Axes of the slice: x: 2, y: 2, z: 4, core: 2. Of those that a mesh axis runs over, the one named last changes fastest.
Arguments:
- cholesky: bfloat16 [2048, 262144], P('narrow', 'wide'), may hold values from -0.015625 to 0.015625
- fields: bfloat16 [2, 32, 2048], P(None, 'wide', 'narrow'), may hold values from -4 to 4
- walkers: bfloat16 [32, 512, 128], P(('wide', 'narrow')), may hold values from -5 to 5
- one_body: bfloat16 [512, 512], replicated, may hold values from -0.078125 to 1
Outputs:
- propagated: bfloat16 [32, 512, 128], P(('wide', 'narrow'))
The draws below stay inside these ranges and needn't reach their ends.
All inputs are finite; a program needn't handle non-finite values.
Results may differ from the reference program's by a relative error of at most 0.024.
Values may be sent and summed in bfloat16 or wider, within the bound.
A program may use at most 128 MiB of HBM per device.

```python
import jax
import jax.numpy as jnp
from jax import lax

NORB = 512
NE = 64
NCHOL = 2048
STEPS = 2
ORDER = 6
WALKERS = 32
CHOL_DEV = 512
N_NARROW = 4


def draw_one_body(key, part):
    key_off, key_diag = jax.random.split(jax.random.fold_in(key, 17), 2)
    spread = 0.2
    lowest = 0.7
    entries = jax.random.normal(key_off, (NORB, NORB), jnp.float32)
    symmetric = (entries + entries.T) * (spread / (2.0 * NORB) ** 0.5)
    symmetric = jnp.clip(symmetric, -0.078125, 0.078125)
    diagonal = jax.random.uniform(key_diag, (NORB,), jnp.float32, lowest, 1.0)
    identity = jnp.eye(NORB, dtype=jnp.float32)
    return (symmetric * (1.0 - identity) + identity * diagonal[:, None]).astype(jnp.bfloat16)


def block_scale(stream_key, shape, cuts, least, largest):
    def one(dim, parts):
        draws = jax.random.uniform(jax.random.fold_in(jax.random.fold_in(stream_key, 6), dim), (parts,), jnp.float32, least / len(cuts), largest / len(cuts))
        return jnp.repeat(jnp.exp(draws), shape[dim] // parts).reshape((-1,) + (1,) * (len(shape) - dim - 1))

    gain = one(*cuts[0])
    for cut in cuts[1:]:
        gain = gain * one(*cut)
    return gain


def noise(stream_key, extent, scale, bound, cuts=(), kind=jnp.bfloat16):
    array = jax.random.normal(stream_key, extent, jnp.float32) * scale
    if len(cuts) > 0:
        array = block_scale(stream_key, extent, cuts, -0.22, 0.18) * array
    return jnp.clip(array, min=-bound, max=bound).astype(kind)


def setup_inputs(seed: int = 0) -> dict:
    seeds = jax.random.split(jax.random.key(seed), 5)
    cholesky = noise(seeds[0], (NCHOL, NORB * NORB), (1.06 / (NORB * NCHOL) ** 0.5), 0.015625, ((0, 4), (1, 8)))
    fields = noise(seeds[1], (STEPS, WALKERS, NCHOL), 1.0, 4.0, ((1, 8), (2, 4)))
    walkers = noise(seeds[2], (WALKERS, NORB, 2 * NE), 1.0, 5.0, ((0, 32),))
    one_body = draw_one_body(jax.random.fold_in(seeds[4], 71), 0)
    return {"cholesky": cholesky, "fields": fields, "walkers": walkers, "one_body": one_body}


def taylor_apply(propagator, walker, one_body):
    half_cols = walker.shape[1] // 2
    term_now = walker
    summed = walker.astype(jnp.float32)
    for order_index in range(1, ORDER + 1):
        direct_part = jnp.dot(propagator, term_now, preferred_element_type=jnp.float32)
        mirror_part = jnp.dot(propagator.T, term_now, preferred_element_type=jnp.float32)
        product = (direct_part + mirror_part) / order_index
        rotated = jnp.concatenate((-product[:, half_cols:], product[:, :half_cols]), axis=1)
        summed = summed + rotated
        term_now = rotated.astype(jnp.bfloat16)
    stepped = summed.astype(jnp.bfloat16)
    return jnp.dot(one_body, stepped, preferred_element_type=jnp.float32).astype(jnp.bfloat16)


def reference(cholesky, fields, walkers, one_body):
    current = walkers
    for step_index in range(STEPS):
        field_now = fields[step_index]
        summed = jnp.zeros((WALKERS, NORB * NORB), jnp.float32)
        for block_index in range(N_NARROW):
            lower_row = block_index * CHOL_DEV
            partial_value = jnp.dot(field_now[:, lower_row:lower_row + CHOL_DEV], cholesky[lower_row:lower_row + CHOL_DEV], preferred_element_type=jnp.float32)
            partial_value = lax.optimization_barrier(partial_value.astype(jnp.bfloat16))
            summed = summed + partial_value.astype(jnp.float32)
        propagator = summed.astype(jnp.bfloat16).reshape(WALKERS, NORB, NORB)

        def advance(operands):
            matrix_in, walker = operands
            return taylor_apply(matrix_in, walker, one_body)

        current = lax.map(advance, (propagator, current))
    return current
```

```python
import functools

import jax
import jax.numpy as jnp
from jax import lax
from jax.experimental import pallas as pl
from jax.experimental.pallas import tpu as pltpu
from jax.sharding import PartitionSpec as P

ORDER = 6
SUB = 8
MIB = 1024 * 1024


def rotation_table(columns):
    half_cols = columns // 2
    source = lax.broadcasted_iota(jnp.int32, (columns, columns), 0)
    target = lax.broadcasted_iota(jnp.int32, (columns, columns), 1)
    negative = jnp.where((target < half_cols) & (source == target + half_cols), -1.0, 0.0)
    positive = jnp.where((target >= half_cols) & (source == target - half_cols), 1.0, 0.0)
    return (negative + positive).astype(jnp.bfloat16)


def advance(propagator, current, one_body):
    rotation = rotation_table(current.shape[2])
    both_sides = jnp.concatenate((propagator, jnp.swapaxes(propagator, 1, 2)), axis=2)
    term_now = current
    summed = current.astype(jnp.float32)
    for order_index in range(1, ORDER + 1):
        turned = jnp.einsum(
            "wqe,ef->wqf", term_now, rotation, preferred_element_type=jnp.float32
        ).astype(jnp.bfloat16)
        doubled = jnp.concatenate((turned, turned), axis=1)
        rotated = (
            jnp.einsum("wpq,wqe->wpe", both_sides, doubled, preferred_element_type=jnp.float32)
            / order_index
        )
        summed = summed + rotated
        term_now = rotated.astype(jnp.bfloat16)
    stepped = summed.astype(jnp.bfloat16)
    return jnp.einsum("pq,wqe->wpe", one_body, stepped, preferred_element_type=jnp.float32).astype(
        jnp.bfloat16
    )


def general(cholesky, fields, walkers, one_body):
    wide_count = lax.axis_size("wide")
    narrow_count = lax.axis_size("narrow")
    every_field = lax.all_gather(fields, "wide", axis=1, tiled=True)
    steps_total, walker_total, chol_rows = every_field.shape
    local_walkers, orbitals, columns = walkers.shape
    pair_cols = cholesky.shape[1]
    ordered = every_field.reshape(steps_total, wide_count, narrow_count, local_walkers, chol_rows)
    ordered = ordered.transpose(2, 0, 1, 3, 4).reshape(steps_total * walker_total, chol_rows)
    summed = lax.psum_scatter(
        jnp.dot(ordered, cholesky, preferred_element_type=jnp.float32).astype(jnp.bfloat16),
        "narrow",
        scatter_dimension=0,
        tiled=True,
    )
    tile_rows = summed.reshape(steps_total, wide_count, local_walkers, pair_cols)
    received = lax.all_to_all(tile_rows, "wide", split_axis=1, concat_axis=1, tiled=True)
    count_items = received.shape[0]
    propagators = received.transpose(0, 2, 1, 3).reshape(
        count_items, local_walkers, orbitals, orbitals
    )
    current = walkers
    for step_index in range(steps_total):
        current = advance(propagators[step_index], current, one_body)
    return current


def build_kernel(
    wide, steps, orbitals, chunks,
    fields_ref, chol_hbm, prop_ref,
    chol, gathered, lhs, keep, send1, recv1, send2, recv2, fin32, fin16,
    chol_sem, gs_sem, gr_sem, s1_sem, r1_sem, s2_sem, r2_sem, fs_sem, fr_sem,
):
    me = lax.axis_index("wide")
    near = lax.axis_index("narrow")
    row, col = lax.div(near, 2), lax.rem(near, 2)
    across_x = row * 2 + (1 - col)
    across_y = (1 - row) * 2 + col
    cols = SUB * orbitals
    group = steps * wide
    blocks = chunks // 2
    tile = 2 * orbitals

    def chol_copy(k):
        return pltpu.make_async_copy(
            chol_hbm.at[:, pl.ds(k * cols, cols)], chol.at[k], chol_sem.at[k]
        )

    for k in range(chunks):
        chol_copy(k).start()

    def peer(d):
        return lax.rem(me + d, wide)

    barrier = pltpu.get_barrier_semaphore()
    for d in range(1, wide):
        pl.semaphore_signal(barrier, inc=1, device_id=(peer(d), near))
    pl.semaphore_signal(barrier, inc=1, device_id=(me, across_x))
    pl.semaphore_signal(barrier, inc=1, device_id=(me, across_y))
    pl.semaphore_wait(barrier, wide + 1)

    def field_copy(d):
        return pltpu.make_async_remote_copy(
            src_ref=fields_ref, dst_ref=gathered.at[me],
            send_sem=gs_sem.at[d], recv_sem=gr_sem.at[d], device_id=(peer(d), near),
        )

    def field_arrival(d):
        return pltpu.make_async_remote_copy(
            src_ref=fields_ref, dst_ref=gathered.at[peer(wide - d)],
            send_sem=gs_sem.at[d], recv_sem=gr_sem.at[d], device_id=(peer(d), near),
        )

    for d in range(1, wide):
        field_copy(d).start()
    gathered[me] = fields_ref[...]
    for d in range(1, wide):
        field_arrival(d).wait_recv()

    for g in range(4):
        rows = jnp.concatenate(
            [gathered[:, g * steps + s, :] for s in range(steps)], axis=0
        ).astype(jnp.bfloat16)
        swapped = (0, 2, 1, 3)[g]
        lhs[0, swapped * group:(swapped + 1) * group, :] = rows
        lhs[1, g * group:(g + 1) * group, :] = rows

    def first_copy(k):
        return pltpu.make_async_remote_copy(
            src_ref=send1.at[k], dst_ref=recv1.at[k], send_sem=s1_sem.at[k], recv_sem=r1_sem.at[k],
            device_id=(me, across_x if k % 2 == 0 else across_y),
        )

    def second_copy(k):
        return pltpu.make_async_remote_copy(
            src_ref=send2.at[k], dst_ref=recv2.at[k], send_sem=s2_sem.at[k], recv_sem=r2_sem.at[k],
            device_id=(me, across_y if k % 2 == 0 else across_x),
        )

    def multiply(k):
        chol_copy(k).wait()

        @pl.loop(0, cols // tile)
        def _(i):
            span = pl.ds(pl.multiple_of(i * tile, tile), tile)
            part = jnp.dot(lhs[k % 2], chol[k, :, span], preferred_element_type=jnp.float32)
            keep[k, :, span] = part[:2 * group]
            send1[k, :, span] = part[2 * group:].astype(jnp.bfloat16)

        first_copy(k).start()

    def middle(k):
        first_copy(k).wait_recv()

        @pl.loop(0, cols // tile)
        def _(i):
            span = pl.ds(pl.multiple_of(i * tile, tile), tile)
            part = keep[k, :, span] + recv1[k, :, span].astype(jnp.float32)
            keep[k, :group, span] = part[:group]
            send2[k, :, span] = part[group:].astype(jnp.bfloat16)

        second_copy(k).start()

    def last_copy(j, d):
        return pltpu.make_async_remote_copy(
            src_ref=fin16.at[j, peer(d)], dst_ref=prop_ref.at[:, me * blocks + j],
            send_sem=fs_sem.at[j, d], recv_sem=fr_sem.at[j, d], device_id=(peer(d), near),
        )

    def last_arrival(j, d):
        return pltpu.make_async_remote_copy(
            src_ref=fin16.at[j, peer(d)], dst_ref=prop_ref.at[:, peer(wide - d) * blocks + j],
            send_sem=fs_sem.at[j, d], recv_sem=fr_sem.at[j, d], device_id=(peer(d), near),
        )

    def finish(j):
        for half in range(2):
            k = 2 * j + half
            second_copy(k).wait_recv()
            for p in range(SUB):
                span = pl.ds(p * orbitals, orbitals)
                fin32[:, half * SUB + p, :] = (
                    keep[k, :group, span] + recv2[k, :, span].astype(jnp.float32)
                )
        for s in range(steps):
            for w in range(wide):
                fin16[j, w, s] = fin32[s * wide + w].astype(jnp.bfloat16)
        for d in range(1, wide):
            last_copy(j, d).start()
        prop_ref[:, me * blocks + j] = fin16[j, me]

    for t in range(chunks + 5):
        if t < chunks:
            multiply(t)
        if 0 <= t - 3 < chunks:
            middle(t - 3)
        if t - 5 >= 0 and (t - 5) % 2 == 1:
            finish((t - 5) // 2)
    for j in range(blocks):
        for d in range(1, wide):
            last_arrival(j, d).wait_recv()
    for d in range(1, wide):
        field_copy(d).wait_send()
    for k in range(chunks):
        first_copy(k).wait_send()
        second_copy(k).wait_send()
    for j in range(blocks):
        for d in range(1, wide):
            last_copy(j, d).wait_send()


def taylor_kernel(steps, prop_ref, walker_ref, body_ref, out_ref):
    columns = walker_ref.shape[1]
    half_cols = columns // 2
    lane = lax.broadcasted_iota(jnp.int32, (1, columns), 1)
    sign = jnp.where(lane < half_cols, -1.0, 1.0).astype(jnp.float32)
    sides = []
    for s in range(steps):
        wider = prop_ref[s].astype(jnp.float32)
        sides.append((wider + wider.T).astype(jnp.bfloat16))
    current = walker_ref[...]
    for s in range(steps):
        term_now = current
        summed = current.astype(jnp.float32)
        for order_index in range(1, ORDER + 1):
            product = jnp.dot(sides[s], term_now, preferred_element_type=jnp.float32)
            rotated = pltpu.roll(product, half_cols, 1) * (sign * (1.0 / order_index))
            summed = summed + rotated
            term_now = rotated.astype(jnp.bfloat16)
        current = jnp.dot(
            body_ref[...], summed.astype(jnp.bfloat16), preferred_element_type=jnp.float32
        ).astype(jnp.bfloat16)
    out_ref[...] = current


def local(cholesky, fields, walkers, one_body):
    wide = lax.axis_size("wide")
    steps, _, depth = fields.shape
    _, orbitals, columns = walkers.shape
    pair_cols = cholesky.shape[1]
    near = lax.axis_index("narrow")
    row, col = near // 2, near % 2
    grid = fields.astype(jnp.float32).reshape(steps, 2, 2, depth)
    grid = jnp.where(row == 1, grid[:, ::-1], grid)
    grid = jnp.where(col == 1, grid[:, :, ::-1], grid)
    relative = grid.transpose(1, 2, 0, 3).reshape(4 * steps, depth)

    chunk_cols = SUB * orbitals
    chunks = pair_cols // chunk_cols
    blocks = chunks // 2
    group = steps * wide
    vmem, dma = pltpu.VMEM, pltpu.SemaphoreType.DMA
    bf16, f32 = jnp.bfloat16, jnp.float32
    props = pl.pallas_call(
        functools.partial(build_kernel, wide, steps, orbitals, chunks),
        out_shape=jax.ShapeDtypeStruct((steps, wide * blocks, 2 * SUB, orbitals), bf16),
        in_specs=[pl.BlockSpec(memory_space=pltpu.VMEM), pl.BlockSpec(memory_space=pl.ANY)],
        out_specs=pl.BlockSpec(memory_space=pltpu.VMEM),
        scratch_shapes=[
            vmem((chunks, depth, chunk_cols), bf16),
            vmem((wide, 4 * steps, depth), f32),
            vmem((2, 4 * group, depth), bf16),
            vmem((chunks, 2 * group, chunk_cols), f32),
            vmem((chunks, 2 * group, chunk_cols), bf16),
            vmem((chunks, 2 * group, chunk_cols), bf16),
            vmem((chunks, group, chunk_cols), bf16),
            vmem((chunks, group, chunk_cols), bf16),
            vmem((group, 2 * SUB, orbitals), f32),
            vmem((blocks, wide, steps, 2 * SUB, orbitals), bf16),
            dma((chunks,)),
            dma((wide,)), dma((wide,)),
            dma((chunks,)), dma((chunks,)), dma((chunks,)), dma((chunks,)),
            dma((blocks, wide)), dma((blocks, wide)),
        ],
        compiler_params=pltpu.CompilerParams(
            collective_id=0, has_side_effects=True, vmem_limit_bytes=56 * MIB
        ),
        name="propagators",
    )(relative, cholesky)
    moved = pl.pallas_call(
        functools.partial(taylor_kernel, steps),
        out_shape=jax.ShapeDtypeStruct((orbitals, columns), bf16),
        in_specs=[pl.BlockSpec(memory_space=pltpu.VMEM)] * 3,
        out_specs=pl.BlockSpec(memory_space=pltpu.VMEM),
        compiler_params=pltpu.CompilerParams(vmem_limit_bytes=32 * MIB),
        name="taylor",
    )(props.reshape(steps, orbitals, orbitals), walkers[0], one_body)
    return moved[None]


def solution(mesh):
    def choose(cholesky, fields, walkers, one_body):
        _, orbitals, _ = walkers.shape
        pair_cols = cholesky.shape[1]
        group = fields.shape[0] * lax.axis_size("wide")
        fits = (
            lax.axis_size("narrow") == 4
            and walkers.shape[0] == 1
            and group % 16 == 0
            and pair_cols % (2 * SUB * orbitals) == 0
            and cholesky.shape[0] * pair_cols * 2 <= 32 * MIB
        )
        return (local if fits else general)(cholesky, fields, walkers, one_body)

    return jax.shard_map(
        choose,
        mesh=mesh,
        in_specs=(
            P("narrow", "wide"),
            P(None, "wide", "narrow"),
            P(("wide", "narrow"), None, None),
            P(),
        ),
        out_specs=P(("wide", "narrow"), None, None),
        check_vma=False,
    )
```

```python
import functools

import jax
import jax.numpy as jnp
from jax import lax
from jax.experimental import pallas as pl
from jax.experimental.pallas import tpu as pltpu
from jax.sharding import PartitionSpec as P

ORDER = 6
SUB = 8
MIB = 1024 * 1024


def rotation_table(columns):
    half_cols = columns // 2
    source = lax.broadcasted_iota(jnp.int32, (columns, columns), 0)
    target = lax.broadcasted_iota(jnp.int32, (columns, columns), 1)
    negative = jnp.where((target < half_cols) & (source == target + half_cols), -1.0, 0.0)
    positive = jnp.where((target >= half_cols) & (source == target - half_cols), 1.0, 0.0)
    return (negative + positive).astype(jnp.bfloat16)


def advance(propagator, current, one_body):
    rotation = rotation_table(current.shape[2])
    both_sides = jnp.concatenate((propagator, jnp.swapaxes(propagator, 1, 2)), axis=2)
    term_now = current
    summed = current.astype(jnp.float32)
    for order_index in range(1, ORDER + 1):
        turned = jnp.einsum(
            "wqe,ef->wqf", term_now, rotation, preferred_element_type=jnp.float32
        ).astype(jnp.bfloat16)
        doubled = jnp.concatenate((turned, turned), axis=1)
        rotated = (
            jnp.einsum("wpq,wqe->wpe", both_sides, doubled, preferred_element_type=jnp.float32)
            / order_index
        )
        summed = summed + rotated
        term_now = rotated.astype(jnp.bfloat16)
    stepped = summed.astype(jnp.bfloat16)
    return jnp.einsum("pq,wqe->wpe", one_body, stepped, preferred_element_type=jnp.float32).astype(
        jnp.bfloat16
    )


def general(cholesky, fields, walkers, one_body):
    wide_count = lax.axis_size("wide")
    narrow_count = lax.axis_size("narrow")
    every_field = lax.all_gather(fields, "wide", axis=1, tiled=True)
    steps_total, walker_total, chol_rows = every_field.shape
    local_walkers, orbitals, columns = walkers.shape
    pair_cols = cholesky.shape[1]
    ordered = every_field.reshape(steps_total, wide_count, narrow_count, local_walkers, chol_rows)
    ordered = ordered.transpose(2, 0, 1, 3, 4).reshape(steps_total * walker_total, chol_rows)
    summed = lax.psum_scatter(
        jnp.dot(ordered, cholesky, preferred_element_type=jnp.float32).astype(jnp.bfloat16),
        "narrow",
        scatter_dimension=0,
        tiled=True,
    )
    tile_rows = summed.reshape(steps_total, wide_count, local_walkers, pair_cols)
    received = lax.all_to_all(tile_rows, "wide", split_axis=1, concat_axis=1, tiled=True)
    count_items = received.shape[0]
    propagators = received.transpose(0, 2, 1, 3).reshape(
        count_items, local_walkers, orbitals, orbitals
    )
    current = walkers
    for step_index in range(steps_total):
        current = advance(propagators[step_index], current, one_body)
    return current


def propagate_kernel(
    wide, steps, orbitals, chunks,
    fields_ref, chol_hbm, walker_ref, body_ref, out_ref,
    chol, own, gathered, lhs, keep, send1, recv1, send2, recv2, fin32, fin16, prop,
    chol_sem, gs_sem, gr_sem, s1_sem, r1_sem, s2_sem, r2_sem, fs_sem, fr_sem,
):
    me = lax.axis_index("wide")
    near = lax.axis_index("narrow")
    row, col = lax.div(near, 2), lax.rem(near, 2)
    across_x = row * 2 + (1 - col)
    across_y = (1 - row) * 2 + col
    cols = SUB * orbitals
    both = 2 * wide
    blocks = chunks // 2
    tile = 2 * orbitals
    ahead = 3

    def chol_copy(k):
        return pltpu.make_async_copy(
            chol_hbm.at[:, pl.ds(k * cols, cols)], chol.at[k], chol_sem.at[k]
        )

    for k in range(min(ahead, chunks)):
        chol_copy(k).start()

    def peer(d):
        return lax.rem(me + d, wide)

    barrier = pltpu.get_barrier_semaphore()
    for d in range(1, wide):
        pl.semaphore_signal(barrier, inc=1, device_id=(peer(d), near))
    pl.semaphore_signal(barrier, inc=1, device_id=(me, across_x))
    pl.semaphore_signal(barrier, inc=1, device_id=(me, across_y))

    mine = fields_ref[...].astype(jnp.float32)
    for s in range(steps):
        for a in range(2):
            for b in range(2):
                def pick(y, x):
                    return mine[s, 2 * y + x:2 * y + x + 1, :]

                upper = jnp.where(col == 0, pick(a, b), pick(a, 1 - b))
                lower = jnp.where(col == 0, pick(1 - a, b), pick(1 - a, 1 - b))
                at = (2 * a + b) * steps + s
                own[at:at + 1, :] = jnp.where(row == 0, upper, lower)
    pl.semaphore_wait(barrier, wide + 1)

    def field_copy(d, source):
        return pltpu.make_async_remote_copy(
            src_ref=own, dst_ref=gathered.at[source],
            send_sem=gs_sem.at[d], recv_sem=gr_sem.at[d], device_id=(peer(d), near),
        )

    for d in range(1, wide):
        field_copy(d, me).start()
    for k in range(ahead, min(ahead + 2, chunks)):
        chol_copy(k).start()
    gathered[me] = own[...]
    for d in range(1, wide):
        field_copy(d, peer(wide - d)).wait_recv()

    for path, order in enumerate(((0, 2, 1, 3), (0, 1, 2, 3))):
        for role in range(2):
            first, second = order[2 * role:2 * role + 2]
            for s in range(steps):
                at = (role * steps + s) * both
                lhs[path, at:at + both, :] = jnp.concatenate(
                    [gathered[:, first * steps + s, :], gathered[:, second * steps + s, :]], axis=0
                ).astype(jnp.bfloat16)

    def first_copy(s, k):
        return pltpu.make_async_remote_copy(
            src_ref=send1.at[s, k], dst_ref=recv1.at[s, k],
            send_sem=s1_sem.at[s, k], recv_sem=r1_sem.at[s, k],
            device_id=(me, across_x if k % 2 == 0 else across_y),
        )

    def second_copy(s, k):
        return pltpu.make_async_remote_copy(
            src_ref=send2.at[s, k], dst_ref=recv2.at[s, k],
            send_sem=s2_sem.at[s, k], recv_sem=r2_sem.at[s, k],
            device_id=(me, across_y if k % 2 == 0 else across_x),
        )

    def multiply(k):
        chol_copy(k).wait()
        if k + ahead + 2 < chunks:
            chol_copy(k + ahead + 2).start()

        @pl.loop(0, cols // tile)
        def _(i):
            span = pl.ds(pl.multiple_of(i * tile, tile), tile)
            part = jnp.dot(lhs[k % 2], chol[k, :, span], preferred_element_type=jnp.float32)
            for s in range(steps):
                keep[s, k, :, span] = part[s * both:(s + 1) * both]
                send1[s, k, :, span] = part[
                    (steps + s) * both:(steps + s + 1) * both
                ].astype(jnp.bfloat16)

    def middle(s, k):
        first_copy(s, k).wait_recv()

        @pl.loop(0, cols // (2 * tile))
        def _(i):
            outgoing = []
            for half in range(2):
                start = pl.multiple_of(half * (cols // 2) + i * tile, tile)
                span = pl.ds(start, tile)
                part = keep[s, k, :, span] + recv1[s, k, :, span].astype(jnp.float32)
                keep[s, k, :wide, span] = part[:wide]
                outgoing.append(part[wide:])
            span = pl.ds(pl.multiple_of(i * tile, tile), tile)
            send2[s, k, :, span] = jnp.concatenate(outgoing, axis=0).astype(jnp.bfloat16)

        second_copy(s, k).start()

    def last_copy(s, j, d, source):
        return pltpu.make_async_remote_copy(
            src_ref=fin16.at[s, j, peer(d)], dst_ref=prop.at[s, source * blocks + j],
            send_sem=fs_sem.at[s, j, d], recv_sem=fr_sem.at[s, j, d], device_id=(peer(d), near),
        )

    def finish(s, j):
        for half in range(2):
            k = 2 * j + half
            second_copy(s, k).wait_recv()
            for p in range(SUB // 2):
                later = p + SUB // 2
                span = pl.ds(p * orbitals, orbitals)
                arrived = recv2[s, k, :, span].astype(jnp.float32)
                fin32[:, half * SUB + p, :] = keep[s, k, :wide, span] + arrived[:wide]
                fin32[:, half * SUB + later, :] = (
                    keep[s, k, :wide, pl.ds(later * orbitals, orbitals)] + arrived[wide:]
                )
        for w in range(wide):
            fin16[s, j, w] = fin32[w].astype(jnp.bfloat16)
        for d in range(1, wide):
            last_copy(s, j, d, me).start()
        prop[s, me * blocks + j] = fin16[s, j, me]

    columns = walker_ref.shape[1]
    half_cols = columns // 2
    lane = lax.broadcasted_iota(jnp.int32, (1, columns), 1)
    sign = jnp.where(lane < half_cols, -1.0, 1.0).astype(jnp.float32)

    def taylor(s):
        for j in range(blocks):
            for d in range(1, wide):
                last_copy(s, j, d, peer(wide - d)).wait_recv()
        wider = prop[s].reshape(orbitals, orbitals).astype(jnp.float32)
        sides = (wider + wider.T).astype(jnp.bfloat16)
        term_now = walker_ref[...] if s == 0 else out_ref[...]
        summed = term_now.astype(jnp.float32)
        for order_index in range(1, ORDER + 1):
            product = jnp.dot(sides, term_now, preferred_element_type=jnp.float32)
            rotated = pltpu.roll(product, half_cols, 1) * (sign * (1.0 / order_index))
            summed = summed + rotated
            term_now = rotated.astype(jnp.bfloat16)
        out_ref[...] = jnp.dot(
            body_ref[...], summed.astype(jnp.bfloat16), preferred_element_type=jnp.float32
        ).astype(jnp.bfloat16)

    early = 2
    finished = 0
    for k in range(chunks):
        multiply(k)
        for s in range(steps if k < early else 1):
            first_copy(s, k).start()
        if k >= 3:
            middle(0, k - 3)
        if k >= 6 and k % 2 == 0:
            finish(0, finished)
            finished += 1
    waiting = [(s, k) for s in range(1, steps) for k in range(early, chunks)]
    for k in range(max(chunks - 3, 0), chunks):
        for held in waiting[:2]:
            first_copy(*held).start()
        waiting = waiting[2:]
        middle(0, k)
    for held in waiting:
        first_copy(*held).start()
    for s in range(1, steps):
        for k in range(early):
            middle(s, k)
    for j in range(finished, blocks):
        finish(0, j)
    for s in range(1, steps):
        finished = 0
        for k in range(early, chunks):
            if k == chunks - 2:
                taylor(s - 1)
            middle(s, k)
            if k % 2 == 1:
                finish(s, finished)
                finished += 1
        if chunks <= early:
            taylor(s - 1)
        for j in range(finished, blocks):
            finish(s, j)
    taylor(steps - 1)

    for d in range(1, wide):
        field_copy(d, me).wait_send()
    for s in range(steps):
        for k in range(chunks):
            first_copy(s, k).wait_send()
            second_copy(s, k).wait_send()
        for j in range(blocks):
            for d in range(1, wide):
                last_copy(s, j, d, me).wait_send()


def local(cholesky, fields, walkers, one_body):
    wide = lax.axis_size("wide")
    steps, _, depth = fields.shape
    _, orbitals, columns = walkers.shape
    chunk_cols = SUB * orbitals
    chunks = cholesky.shape[1] // chunk_cols
    blocks = chunks // 2
    both = 2 * wide
    vmem, dma = pltpu.VMEM, pltpu.SemaphoreType.DMA
    bf16, f32 = jnp.bfloat16, jnp.float32
    in_vmem = pl.BlockSpec(memory_space=pltpu.VMEM)
    moved = pl.pallas_call(
        functools.partial(propagate_kernel, wide, steps, orbitals, chunks),
        out_shape=jax.ShapeDtypeStruct((orbitals, columns), bf16),
        in_specs=[in_vmem, pl.BlockSpec(memory_space=pl.ANY), in_vmem, in_vmem],
        out_specs=in_vmem,
        scratch_shapes=[
            vmem((chunks, depth, chunk_cols), bf16),
            vmem((4 * steps, depth), f32),
            vmem((wide, 4 * steps, depth), f32),
            vmem((2, 2 * steps * both, depth), bf16),
            vmem((steps, chunks, both, chunk_cols), f32),
            vmem((steps, chunks, both, chunk_cols), bf16),
            vmem((steps, chunks, both, chunk_cols), bf16),
            vmem((steps, chunks, both, chunk_cols // 2), bf16),
            vmem((steps, chunks, both, chunk_cols // 2), bf16),
            vmem((wide, 2 * SUB, orbitals), f32),
            vmem((steps, blocks, wide, 2 * SUB, orbitals), bf16),
            vmem((steps, wide * blocks, 2 * SUB, orbitals), bf16),
            dma((chunks,)),
            dma((wide,)), dma((wide,)),
            dma((steps, chunks)), dma((steps, chunks)),
            dma((steps, chunks)), dma((steps, chunks)),
            dma((steps, blocks, wide)), dma((steps, blocks, wide)),
        ],
        compiler_params=pltpu.CompilerParams(
            collective_id=0, has_side_effects=True, vmem_limit_bytes=58 * MIB
        ),
        name="propagate",
    )(fields, cholesky, walkers[0], one_body)
    return moved[None]


def solution(mesh):
    def choose(cholesky, fields, walkers, one_body):
        _, orbitals, _ = walkers.shape
        pair_cols = cholesky.shape[1]
        both = 2 * lax.axis_size("wide")
        fits = (
            lax.axis_size("narrow") == 4
            and walkers.shape[0] == 1
            and both % 16 == 0
            and pair_cols % (2 * SUB * orbitals) == 0
            and cholesky.shape[0] * pair_cols * 2 <= 32 * MIB
        )
        return (local if fits else general)(cholesky, fields, walkers, one_body)

    return jax.shard_map(
        choose,
        mesh=mesh,
        in_specs=(
            P("narrow", "wide"),
            P(None, "wide", "narrow"),
            P(("wide", "narrow"), None, None),
            P(),
        ),
        out_specs=P(("wide", "narrow"), None, None),
        check_vma=False,
    )
```

```python
import functools

import jax
import jax.numpy as jnp
from jax import lax
from jax.experimental import pallas as pl
from jax.experimental.pallas import tpu as pltpu
from jax.sharding import PartitionSpec as P

ORDER = 6
SUB = 8
MIB = 1024 * 1024


def rotation_table(columns):
    half_cols = columns // 2
    source = lax.broadcasted_iota(jnp.int32, (columns, columns), 0)
    target = lax.broadcasted_iota(jnp.int32, (columns, columns), 1)
    negative = jnp.where((target < half_cols) & (source == target + half_cols), -1.0, 0.0)
    positive = jnp.where((target >= half_cols) & (source == target - half_cols), 1.0, 0.0)
    return (negative + positive).astype(jnp.bfloat16)


def advance(propagator, current, one_body):
    rotation = rotation_table(current.shape[2])
    both_sides = jnp.concatenate((propagator, jnp.swapaxes(propagator, 1, 2)), axis=2)
    term_now = current
    summed = current.astype(jnp.float32)
    for order_index in range(1, ORDER + 1):
        turned = jnp.einsum(
            "wqe,ef->wqf", term_now, rotation, preferred_element_type=jnp.float32
        ).astype(jnp.bfloat16)
        doubled = jnp.concatenate((turned, turned), axis=1)
        rotated = (
            jnp.einsum("wpq,wqe->wpe", both_sides, doubled, preferred_element_type=jnp.float32)
            / order_index
        )
        summed = summed + rotated
        term_now = rotated.astype(jnp.bfloat16)
    stepped = summed.astype(jnp.bfloat16)
    return jnp.einsum("pq,wqe->wpe", one_body, stepped, preferred_element_type=jnp.float32).astype(
        jnp.bfloat16
    )


def general(cholesky, fields, walkers, one_body):
    wide_count = lax.axis_size("wide")
    narrow_count = lax.axis_size("narrow")
    every_field = lax.all_gather(fields, "wide", axis=1, tiled=True)
    steps_total, walker_total, chol_rows = every_field.shape
    local_walkers, orbitals, columns = walkers.shape
    pair_cols = cholesky.shape[1]
    ordered = every_field.reshape(steps_total, wide_count, narrow_count, local_walkers, chol_rows)
    ordered = ordered.transpose(2, 0, 1, 3, 4).reshape(steps_total * walker_total, chol_rows)
    summed = lax.psum_scatter(
        jnp.dot(ordered, cholesky, preferred_element_type=jnp.float32).astype(jnp.bfloat16),
        "narrow",
        scatter_dimension=0,
        tiled=True,
    )
    tile_rows = summed.reshape(steps_total, wide_count, local_walkers, pair_cols)
    received = lax.all_to_all(tile_rows, "wide", split_axis=1, concat_axis=1, tiled=True)
    count_items = received.shape[0]
    propagators = received.transpose(0, 2, 1, 3).reshape(
        count_items, local_walkers, orbitals, orbitals
    )
    current = walkers
    for step_index in range(steps_total):
        current = advance(propagators[step_index], current, one_body)
    return current


def propagate_kernel(
    wide, steps, orbitals, chunks,
    fields_ref, chol_hbm, walker_ref, body_ref, out_ref,
    chol, own, gathered, lhs, keep, send1, recv1, send2, recv2, fin32, fin16, prop,
    chol_sem, gs_sem, gr_sem, s1_sem, r1_sem, s2_sem, r2_sem, fs_sem, fr_sem,
):
    me = lax.axis_index("wide")
    near = lax.axis_index("narrow")
    row, col = lax.div(near, 2), lax.rem(near, 2)
    across_x = row * 2 + (1 - col)
    across_y = (1 - row) * 2 + col
    cols = SUB * orbitals
    both = 2 * wide
    blocks = chunks // 2
    tile = 2 * orbitals
    ahead = 3

    def chol_copy(k):
        return pltpu.make_async_copy(
            chol_hbm.at[:, pl.ds(k * cols, cols)], chol.at[k], chol_sem.at[k]
        )

    for k in range(min(ahead, chunks)):
        chol_copy(k).start()

    def peer(d):
        return lax.rem(me + d, wide)

    barrier = pltpu.get_barrier_semaphore()
    for d in range(1, wide):
        pl.semaphore_signal(barrier, inc=1, device_id=(peer(d), near))
    pl.semaphore_signal(barrier, inc=1, device_id=(me, across_x))
    pl.semaphore_signal(barrier, inc=1, device_id=(me, across_y))

    mine = fields_ref[...].astype(jnp.float32)
    for s in range(steps):
        for a in range(2):
            for b in range(2):
                def pick(y, x):
                    return mine[s, 2 * y + x:2 * y + x + 1, :]

                upper = jnp.where(col == 0, pick(a, b), pick(a, 1 - b))
                lower = jnp.where(col == 0, pick(1 - a, b), pick(1 - a, 1 - b))
                at = (2 * a + b) * steps + s
                own[at:at + 1, :] = jnp.where(row == 0, upper, lower)
    pl.semaphore_wait(barrier, wide + 1)

    def field_copy(d, source):
        return pltpu.make_async_remote_copy(
            src_ref=own, dst_ref=gathered.at[source],
            send_sem=gs_sem.at[d], recv_sem=gr_sem.at[d], device_id=(peer(d), near),
        )

    for d in range(1, wide):
        field_copy(d, me).start()
    for k in range(ahead, min(ahead + 2, chunks)):
        chol_copy(k).start()
    gathered[me] = own[...]
    for d in range(1, wide):
        field_copy(d, peer(wide - d)).wait_recv()

    for path, order in enumerate(((0, 2, 1, 3), (0, 1, 2, 3))):
        for role in range(2):
            first, second = order[2 * role:2 * role + 2]
            for s in range(steps):
                at = (role * steps + s) * both
                lhs[path, at:at + both, :] = jnp.concatenate(
                    [gathered[:, first * steps + s, :], gathered[:, second * steps + s, :]], axis=0
                ).astype(jnp.bfloat16)

    def first_copy(s, k):
        return pltpu.make_async_remote_copy(
            src_ref=send1.at[s, k], dst_ref=recv1.at[s, k],
            send_sem=s1_sem.at[s, k], recv_sem=r1_sem.at[s, k],
            device_id=(me, across_x if k % 2 == 0 else across_y),
        )

    def second_copy(s, k):
        return pltpu.make_async_remote_copy(
            src_ref=send2.at[s, k], dst_ref=recv2.at[s, k],
            send_sem=s2_sem.at[s, k], recv_sem=r2_sem.at[s, k],
            device_id=(me, across_y if k % 2 == 0 else across_x),
        )

    def multiply(k):
        chol_copy(k).wait()
        if k + ahead + 2 < chunks:
            chol_copy(k + ahead + 2).start()

        @pl.loop(0, cols // tile)
        def _(i):
            span = pl.ds(pl.multiple_of(i * tile, tile), tile)
            part = jnp.dot(lhs[k % 2], chol[k, :, span], preferred_element_type=jnp.float32)
            for s in range(steps):
                keep[s, k, :, span] = part[s * both:(s + 1) * both]
                send1[s, k, :, span] = part[
                    (steps + s) * both:(steps + s + 1) * both
                ].astype(jnp.bfloat16)

    def middle(s, k):
        first_copy(s, k).wait_recv()

        @pl.loop(0, cols // (2 * tile))
        def _(i):
            outgoing = []
            for half in range(2):
                start = pl.multiple_of(half * (cols // 2) + i * tile, tile)
                span = pl.ds(start, tile)
                part = keep[s, k, :, span] + recv1[s, k, :, span].astype(jnp.float32)
                keep[s, k, :wide, span] = part[:wide]
                outgoing.append(part[wide:])
            span = pl.ds(pl.multiple_of(i * tile, tile), tile)
            send2[s, k, :, span] = jnp.concatenate(outgoing, axis=0).astype(jnp.bfloat16)

        second_copy(s, k).start()

    def last_copy(s, j, d, source):
        return pltpu.make_async_remote_copy(
            src_ref=fin16.at[s, j, peer(d)], dst_ref=prop.at[s, source * blocks + j],
            send_sem=fs_sem.at[s, j, d], recv_sem=fr_sem.at[s, j, d], device_id=(peer(d), near),
        )

    def finish(s, j):
        for half in range(2):
            k = 2 * j + half
            second_copy(s, k).wait_recv()
            for p in range(SUB // 2):
                later = p + SUB // 2
                span = pl.ds(p * orbitals, orbitals)
                arrived = recv2[s, k, :, span].astype(jnp.float32)
                fin32[:, half * SUB + p, :] = keep[s, k, :wide, span] + arrived[:wide]
                fin32[:, half * SUB + later, :] = (
                    keep[s, k, :wide, pl.ds(later * orbitals, orbitals)] + arrived[wide:]
                )
        for w in range(wide):
            fin16[s, j, w] = fin32[w].astype(jnp.bfloat16)
        for d in range(1, wide):
            last_copy(s, j, d, me).start()
        prop[s, me * blocks + j] = fin16[s, j, me]

    columns = walker_ref.shape[1]
    half_cols = columns // 2
    lane = lax.broadcasted_iota(jnp.int32, (1, columns), 1)
    sign = jnp.where(lane < half_cols, -1.0, 1.0).astype(jnp.float32)

    def taylor(s):
        for j in range(blocks):
            for d in range(1, wide):
                last_copy(s, j, d, peer(wide - d)).wait_recv()
        wider = prop[s].reshape(orbitals, orbitals).astype(jnp.float32)
        sides = (wider + wider.T).astype(jnp.bfloat16)
        term_now = walker_ref[...] if s == 0 else out_ref[...]
        summed = term_now.astype(jnp.float32)
        for order_index in range(1, ORDER + 1):
            product = jnp.dot(sides, term_now, preferred_element_type=jnp.float32)
            rotated = pltpu.roll(product, half_cols, 1) * (sign * (1.0 / order_index))
            summed = summed + rotated
            term_now = rotated.astype(jnp.bfloat16)
        out_ref[...] = jnp.dot(
            body_ref[...], summed.astype(jnp.bfloat16), preferred_element_type=jnp.float32
        ).astype(jnp.bfloat16)

    early = max(chunks - 2, 0)
    finished = 0
    for k in range(chunks):
        multiply(k)
        for s in range(steps if k < early else 1):
            first_copy(s, k).start()
        if k >= 3:
            middle(0, k - 3)
        if k >= 6 and k % 2 == 0:
            finish(0, finished)
            finished += 1
    for s in range(1, steps):
        for k in range(early, chunks):
            first_copy(s, k).start()
    coming = [(1, k) for k in range(chunks)] if steps > 1 else []

    def take(count):
        for item in coming[:count]:
            middle(*item)
        del coming[:count]

    for i, k in enumerate(range(max(chunks - 3, 0), chunks)):
        middle(0, k)
        take(2 if i == 0 else 1)
    if finished < blocks - 1:
        finish(0, finished)
        finished += 1
    take(len(coming) - 1)
    for j in range(finished, blocks - 1):
        finish(0, j)
    take(len(coming))
    finish(0, blocks - 1)
    for s in range(1, steps):
        if s > 1:
            for k in range(chunks):
                middle(s, k)
        for j in range(blocks - 1):
            finish(s, j)
        taylor(s - 1)
        finish(s, blocks - 1)
    taylor(steps - 1)

    for d in range(1, wide):
        field_copy(d, me).wait_send()
    for s in range(steps):
        for k in range(chunks):
            first_copy(s, k).wait_send()
            second_copy(s, k).wait_send()
        for j in range(blocks):
            for d in range(1, wide):
                last_copy(s, j, d, me).wait_send()


def local(cholesky, fields, walkers, one_body):
    wide = lax.axis_size("wide")
    steps, _, depth = fields.shape
    _, orbitals, columns = walkers.shape
    chunk_cols = SUB * orbitals
    chunks = cholesky.shape[1] // chunk_cols
    blocks = chunks // 2
    both = 2 * wide
    vmem, dma = pltpu.VMEM, pltpu.SemaphoreType.DMA
    bf16, f32 = jnp.bfloat16, jnp.float32
    in_vmem = pl.BlockSpec(memory_space=pltpu.VMEM)
    moved = pl.pallas_call(
        functools.partial(propagate_kernel, wide, steps, orbitals, chunks),
        out_shape=jax.ShapeDtypeStruct((orbitals, columns), bf16),
        in_specs=[in_vmem, pl.BlockSpec(memory_space=pl.ANY), in_vmem, in_vmem],
        out_specs=in_vmem,
        scratch_shapes=[
            vmem((chunks, depth, chunk_cols), bf16),
            vmem((4 * steps, depth), f32),
            vmem((wide, 4 * steps, depth), f32),
            vmem((2, 2 * steps * both, depth), bf16),
            vmem((steps, chunks, both, chunk_cols), f32),
            vmem((steps, chunks, both, chunk_cols), bf16),
            vmem((steps, chunks, both, chunk_cols), bf16),
            vmem((steps, chunks, both, chunk_cols // 2), bf16),
            vmem((steps, chunks, both, chunk_cols // 2), bf16),
            vmem((wide, 2 * SUB, orbitals), f32),
            vmem((steps, blocks, wide, 2 * SUB, orbitals), bf16),
            vmem((steps, wide * blocks, 2 * SUB, orbitals), bf16),
            dma((chunks,)),
            dma((wide,)), dma((wide,)),
            dma((steps, chunks)), dma((steps, chunks)),
            dma((steps, chunks)), dma((steps, chunks)),
            dma((steps, blocks, wide)), dma((steps, blocks, wide)),
        ],
        compiler_params=pltpu.CompilerParams(
            collective_id=0, has_side_effects=True, vmem_limit_bytes=58 * MIB
        ),
        name="propagate",
    )(fields, cholesky, walkers[0], one_body)
    return moved[None]


def solution(mesh):
    def choose(cholesky, fields, walkers, one_body):
        _, orbitals, _ = walkers.shape
        pair_cols = cholesky.shape[1]
        both = 2 * lax.axis_size("wide")
        fits = (
            lax.axis_size("narrow") == 4
            and walkers.shape[0] == 1
            and both % 16 == 0
            and pair_cols % (2 * SUB * orbitals) == 0
            and cholesky.shape[0] * pair_cols * 2 <= 32 * MIB
        )
        return (local if fits else general)(cholesky, fields, walkers, one_body)

    return jax.shard_map(
        choose,
        mesh=mesh,
        in_specs=(
            P("narrow", "wide"),
            P(None, "wide", "narrow"),
            P(("wide", "narrow"), None, None),
            P(),
        ),
        out_specs=P(("wide", "narrow"), None, None),
        check_vma=False,
    )
```
